256 devices in a mesh: band: 16 (over x, z_hi), ga: 16 (over z_lo, y, core).
Axes of the slice: x: 4, y: 4, z: 8 (z_hi: 4, z_lo: 2; z = z_hi * 2 + z_lo), core: 2. Of those that a mesh axis runs over, the one named last changes fastest.
Arguments:
- valence_waves: bfloat16 [2, 6, 32, 1024], P(None, None, 'ga'), may hold values from -6 to 6
- conduction_waves: bfloat16 [2, 256, 32, 1024], P(None, 'band', 'ga'), may hold values from -6 to 6
- valence_energy: float32 [6], replicated, may hold values from -2 to 0
- conduction_energy: float32 [256], P('band'), may hold values from 0.5 to 3
- valence_occupied: int32 [6], replicated, may hold values 0 or 1
- conduction_occupied: int32 [256], P('band'), may hold values 0 or 1
- gvec_index: int32 [4096], replicated, may hold values from 0 to 32767, as said below
Outputs:
- chi_zero: float32 [4096, 2, 4096], P('band', None, 'ga')
The draws below stay inside these ranges and needn't reach their ends.
Inputs may be any that keep to these rules, and one draw needn't show every extreme that they name: `gvec_index`: distinct grid indices: the 4096 grid points of smallest length of the signed frequency vector (components above 16 taken minus 32), in order of rising length, ties in random order.
All inputs are finite; a program needn't handle non-finite values. No bound on the sum of `conduction_occupied` on one device may be relied on, other than what follows from the above.
Results may differ from the reference program's by a relative error of at most 0.0048.
Values may be sent and summed in bfloat16 or wider, within the bound.
A program may use at most 128 MiB of HBM per device.

```python
import jax
import jax.numpy as jnp
from jax import lax

NR = 32
NG = 4096
NV = 6
CONDUCTION = 256


def draw_gvec_index(key, part):
    key = jax.random.fold_in(key, 7)
    total = NR * NR * NR
    flat = jnp.arange(total, dtype=jnp.int32)
    comp_x = flat // (NR * NR)
    comp_y = flat // NR % NR
    comp_z = flat % NR
    half = NR // 2
    sign_x = jnp.where(comp_x > half, comp_x - NR, comp_x)
    sign_y = jnp.where(comp_y > half, comp_y - NR, comp_y)
    sign_z = jnp.where(comp_z > half, comp_z - NR, comp_z)
    length = sign_x * sign_x + sign_y * sign_y + sign_z * sign_z
    shuffled = jax.random.permutation(key, total).astype(jnp.int32)
    score = length * total + shuffled
    unused, picked = lax.top_k(-score, NG)
    return picked.astype(jnp.int32)


def set_ends(array, own_key, least, largest):
    extent = array.shape
    index_at = [jax.random.randint(jax.random.fold_in(own_key, axis), (), 0, extent[axis]) for axis in range(len(extent))]
    array = array.at[tuple(index_at)].set(least)
    longest = extent.index(max(extent))
    index_at[longest] = (index_at[longest] + 1) % extent[longest]
    return array.at[tuple(index_at)].set(largest)


def steps_of(key, dims, pieces, least, top_value):
    factor_of = 1.0
    for dim, shards_of in pieces:
        steps = jax.random.uniform(jax.random.fold_in(jax.random.fold_in(key, 6), dim), (shards_of,), jnp.float32, least / len(pieces), top_value / len(pieces))
        factor_of = factor_of * jnp.repeat(jnp.exp(steps), dims[dim] // shards_of).reshape((-1,) + (1,) * (len(dims) - 1 - dim))
    return factor_of


def noise(own_key, dims, scale, reach, cuts=(), kind=jnp.bfloat16):
    level = steps_of(own_key, dims, cuts, -0.22, 0.18) if cuts else 1.0
    drawn = jax.random.normal(own_key, dims, jnp.float32) * scale * level
    return jnp.minimum(jnp.maximum(drawn, -reach), reach).astype(kind)


def setup_inputs(seed: int = 0) -> dict:
    key_of = jax.random.split(jax.random.key(seed), 8)
    valence_waves = noise(key_of[0], (2, NV, NR, NR * NR), 1.0, 6.0, ((2, 16),))
    conduction_waves = noise(key_of[1], (2, CONDUCTION, NR, NR * NR), 1.0, 6.0, ((1, 16), (2, 16)))
    valence_energy = jnp.clip(jax.random.uniform(key_of[2], (NV,), jnp.float32, -2.0, 0.0), -2.0, 0.0)
    conduction_energy = jnp.clip(0.5 + 2.5 * jax.random.uniform(key_of[3], (CONDUCTION,), jnp.float32) ** steps_of(key_of[3], (CONDUCTION,), ((0, 16),), -0.2, 0.2), 0.5, 3.0)
    valence_occupied = set_ends((jax.random.randint(key_of[4], (NV,), 0, 2) < 1).astype(jnp.int32), jax.random.fold_in(key_of[4], 1), 0, 1)
    conduction_occupied = set_ends((jax.random.randint(key_of[5], (CONDUCTION,), 0, 4) < 1).astype(jnp.int32), jax.random.fold_in(key_of[5], 1), 0, 1)
    gvec_index = draw_gvec_index(jax.random.fold_in(key_of[7], 71), 0)
    return dict(valence_waves=valence_waves, conduction_waves=conduction_waves, valence_energy=valence_energy, conduction_energy=conduction_energy, valence_occupied=valence_occupied, conduction_occupied=conduction_occupied, gvec_index=gvec_index)


def pair_spectra(valence_one, waves, gvec_index):
    vr = valence_one[0].astype(jnp.float32)[None]
    vi = valence_one[1].astype(jnp.float32)[None]
    cr = waves[0].astype(jnp.float32)
    ci = waves[1].astype(jnp.float32)
    pair_re = vr * cr + vi * ci
    pair_im = vr * ci - vi * cr
    field = (pair_re + 1j * pair_im).reshape(cr.shape[0], NR, NR, NR)
    spectrum = jnp.fft.fftn(field, axes=(1, 2, 3)).reshape(cr.shape[0], NR * NR * NR)
    picked = jnp.take(spectrum, gvec_index, axis=1) * (float(NR) ** -1.5)
    return jnp.stack([jnp.real(picked), jnp.imag(picked)]).astype(jnp.bfloat16)


def reference(valence_waves, conduction_waves, valence_energy, conduction_energy, valence_occupied, conduction_occupied, gvec_index):
    factor = float(NV * CONDUCTION) ** -0.5

    def one_band(carry, inputs):
        wave_one, energy_one, occupied_one = inputs
        rho = pair_spectra(wave_one, conduction_waves, gvec_index)
        weight = (occupied_one - conduction_occupied).astype(jnp.float32) / (energy_one - conduction_energy) * factor
        scaled = (weight[None, :, None] * rho.astype(jnp.float32)).astype(jnp.bfloat16)
        left_re = jnp.concatenate([scaled[0], scaled[1]], axis=0)
        left_im = jnp.concatenate([scaled[1], -scaled[0]], axis=0)
        right = jnp.concatenate([rho[0], rho[1]], axis=0)
        part_re = jnp.dot(left_re.T, right, preferred_element_type=jnp.float32)
        part_im = jnp.dot(left_im.T, right, preferred_element_type=jnp.float32)
        return carry + jnp.stack([part_re, part_im], axis=1), None

    start = jnp.zeros((NG, 2, NG), jnp.float32)
    result, unused = lax.scan(one_band, start, (jnp.moveaxis(valence_waves, 1, 0), valence_energy, valence_occupied))
    return result
```

```python
import numpy as np
import jax
import jax.numpy as jnp
import ml_dtypes
from jax import lax
from jax.experimental import pallas as pl
from jax.experimental.pallas import tpu as pltpu
from jax.sharding import PartitionSpec as P

NR = 32
NG = 4096
NV = 6
VP = 8
MAIN = 256
REST = 64
MESH = pl.DeviceIdType.MESH
F32 = jnp.float32
BF16 = jnp.bfloat16


def signed(k):
    return np.where(k > NR // 2, k - NR, k)


def sphere():
    flat = np.arange(NR**3)
    comps = [signed(c) for c in (flat // NR**2, flat // NR % NR, flat % NR)]
    length = sum(c * c for c in comps)
    inside = flat[length <= np.sort(length)[NG - 1]]
    return np.unique(inside // NR**2), np.unique(inside % NR**2)


KX, COLS = sphere()
NK = len(KX)
NC = len(COLS)
assert MAIN < NC <= MAIN + REST
ROWS = 2 * NK * VP


def split(table):
    high = table.astype(ml_dtypes.bfloat16)
    low = (table - high.astype(np.float64)).astype(ml_dtypes.bfloat16)
    return np.stack([high, low])


def plane_table():
    yz = np.arange(NR * NR)
    turns = (yz // NR)[:, None] * (COLS // NR)[None] + (yz % NR)[:, None] * (COLS % NR)[None]
    angle = 2.0 * np.pi / NR * (turns % NR)
    table = np.zeros((NR * NR, 2 * (MAIN + REST)))
    for part, values in enumerate((np.cos(angle), np.sin(angle))):
        table[:, part * MAIN : (part + 1) * MAIN] = values[:, :MAIN]
        start = 2 * MAIN + part * REST
        table[:, start : start + NC - MAIN] = values[:, MAIN:]
    return split(table)


def line_table():
    angle = 2.0 * np.pi / NR * (KX[:, None] * np.arange(NR)[None] % NR)
    norm = float(NR) ** -1.5
    same = np.eye(VP)
    return split(np.concatenate([np.kron(np.cos(angle), same), np.kron(np.sin(angle), same)]) * norm)


def column_ids():
    ids = np.full((MAIN + 2 * REST,), -1, np.int32)
    ids[:NC] = COLS
    return np.ascontiguousarray(np.broadcast_to(ids[:, None], (MAIN + 2 * REST, 128)))


PLANE = plane_table()
LINE = line_table()
IDS = column_ids()


def halves(value):
    high = value.astype(BF16)
    return high, (value - high.astype(F32)).astype(BF16)


def mm(left, right):
    return jnp.dot(left, right, preferred_element_type=F32)


def kernel(
    val_ref, cond_ref, plane_ref, line_ref, ids_ref, gvec_ref, weight_ref,
    left_ref, right_ref,
    pair_hi, pair_lo, table, a_send, a_recv, hot, rho_send, scl_send, rho_recv, scl_recv,
    tab_sem, s1, r1, s2, r2, s3, r3, cs, cr, rs, rr,
):
    b = lax.axis_index("band")
    g = lax.axis_index("ga")
    bx, bz = b // 4, b % 4
    gl, gy, gc = g // 8, g // 2 % 4, g % 2

    def band_of(x, z):
        return lax.rem(x + 4, 4) * 4 + lax.rem(z + 4, 4)

    def ga_of(l, y, c):
        return l * 8 + lax.rem(y + 4, 4) * 2 + c

    tab = pltpu.make_async_copy(plane_ref, table, tab_sem)
    tab.start()

    barrier = pltpu.get_barrier_semaphore()
    own = (b == g).astype(jnp.int32)

    def greet(dev):
        pl.semaphore_signal(barrier, inc=1, device_id=dev, device_id_type=MESH)

    def greet_group(d, carry):
        greet((b, lax.rem(g + d, 16)))
        return carry

    lax.fori_loop(1, 16, greet_group, 0)

    def greet_rows(d, carry):
        @pl.when(jnp.logical_or(b != g, d != g))
        def _():
            greet((g, d))

        return carry

    lax.fori_loop(0, 16, greet_rows, 0)
    for dx, dz in ((1, 0), (-1, 0), (0, 1), (0, -1)):
        greet((band_of(bx + dx, bz + dz), g))

    cr_all = cond_ref[0].astype(F32)
    ci_all = cond_ref[1].astype(F32)
    vr_all = val_ref[0].astype(F32)
    vi_all = val_ref[1].astype(F32)
    for c in range(16):
        parts_re = []
        parts_im = []
        for plane in range(2):
            row = 2 * c + plane
            cre = cr_all[row : row + 1]
            cim = ci_all[row : row + 1]
            vre = vr_all[plane * VP : (plane + 1) * VP]
            vim = vi_all[plane * VP : (plane + 1) * VP]
            parts_re.append(vre * cre + vim * cim)
            parts_im.append(vre * cim - vim * cre)
        for part, values in enumerate((parts_re, parts_im)):
            high, low = halves(jnp.concatenate(values, axis=0))
            at = part * 256 + 16 * c
            pair_hi[at : at + 16] = high
            pair_lo[at : at + 16] = low

    tab.wait()

    lane = lax.broadcasted_iota(jnp.int32, (1, 128), 1)
    sign = jnp.where(lane < REST, 1.0, -1.0).astype(F32)

    def plane_turn(q, carry):
        def spectra(part):
            at = pl.ds(pl.multiple_of(part * 256 + q * 64, 64), 64)
            return mm(pair_hi[at], table[0]) + mm(pair_lo[at], table[0]) + mm(pair_hi[at], table[1])

        yre = spectra(0)
        yim = spectra(1)
        out = jnp.concatenate(
            [
                yre[:, :MAIN] + yim[:, MAIN : 2 * MAIN],
                yim[:, :MAIN] - yre[:, MAIN : 2 * MAIN],
                pltpu.roll(yim[:, 2 * MAIN :], REST, 1) + sign * yre[:, 2 * MAIN :],
            ],
            axis=1,
        )
        a_send[pl.ds(q * 4, 4)] = out.reshape(4, 16, 640)
        return carry

    lax.fori_loop(0, 4, plane_turn, 0)

    pl.semaphore_wait(barrier, 35 - own)

    def first(dest, slot):
        return pltpu.make_async_remote_copy(
            src_ref=a_send.at[dest], dst_ref=a_recv.at[slot], send_sem=s1.at[dest], recv_sem=r1.at[slot],
            device_id=(b, dest), device_id_type=MESH,
        )

    def send_first(d, carry):
        first(lax.rem(g + d, 16), g).start()
        return carry

    lax.fori_loop(1, 16, send_first, 0)
    a_recv[g] = a_send[g]

    ids = jnp.concatenate([ids_ref[...]] * 2, axis=1)

    def one_hot(j, carry):
        yz = jnp.bitwise_and(gvec_ref[j, 0:1], NR * NR - 1)
        hot[j] = jnp.where(ids == yz, 1.0, 0.0).astype(BF16)
        return carry

    lax.fori_loop(0, 16, one_hot, 0)

    def wait_first(d, carry):
        peer = lax.rem(g + d, 16)
        first(peer, peer).wait_recv()
        return carry

    lax.fori_loop(1, 16, wait_first, 0)

    a_hi, a_lo = halves(a_recv[...].reshape(256, 640))
    uv = mm(line_ref[0], a_hi) + mm(line_ref[0], a_lo) + mm(line_ref[1], a_hi)
    u, v = uv[: ROWS // 2], uv[ROWS // 2 :]
    rest = u[:, 2 * MAIN :] + sign * pltpu.roll(v[:, 2 * MAIN :], REST, 1)
    z_re = jnp.concatenate([u[:, :MAIN] + v[:, MAIN : 2 * MAIN], rest], axis=1)
    z_im = jnp.concatenate([u[:, MAIN : 2 * MAIN] - v[:, :MAIN], pltpu.roll(rest, REST, 1)], axis=1)
    z = jnp.concatenate([z_re, z_im], axis=0).astype(BF16)
    weight = jnp.concatenate([weight_ref[...]] * 2, axis=1)

    def pick(j, carry):
        found = mm(z, hot[j])
        kx = jnp.right_shift(gvec_ref[j], 10)
        re = jnp.zeros((VP, 256), F32)
        im = jnp.zeros((VP, 256), F32)
        for k in range(NK):
            here = kx == int(KX[k])
            re = jnp.where(here, found[k * VP : (k + 1) * VP], re)
            im = jnp.where(here, found[(NK + k) * VP : (NK + k + 1) * VP], im)
        rho_send[j] = jnp.concatenate([re, im], axis=0).astype(BF16)
        scl_send[j] = jnp.concatenate([re * weight, im * weight], axis=0).astype(BF16)
        return carry

    lax.fori_loop(0, 16, pick, 0)

    def second(dest, slot):
        return pltpu.make_async_remote_copy(
            src_ref=rho_send.at[dest], dst_ref=rho_recv.at[slot], send_sem=s2.at[dest], recv_sem=r2.at[slot],
            device_id=(b, dest), device_id_type=MESH,
        )

    def third(dest, slot):
        return pltpu.make_async_remote_copy(
            src_ref=scl_send.at[dest], dst_ref=scl_recv.at[slot], send_sem=s3.at[dest], recv_sem=r3.at[slot],
            device_id=(dest, b), device_id_type=MESH,
        )

    def send_second(d, carry):
        second(lax.rem(g + d, 16), g).start()
        return carry

    def send_third(d, carry):
        dest = lax.rem(b + d, 16)

        @pl.when(jnp.logical_or(b != g, d != 0))
        def _():
            third(dest, g).start()

        return carry

    lax.fori_loop(1, 16, send_second, 0)
    lax.fori_loop(0, 16, send_third, 0)
    rho_recv[g] = rho_send[g]

    @pl.when(b == g)
    def _():
        scl_recv[g] = scl_send[g]

    row = lax.broadcasted_iota(jnp.int32, (VP, 256), 0)

    def repack(src, out, slot):
        for part in range(2):
            groups = []
            for quad in range(4):
                four = [src[4 * quad + i].astype(F32)[part * VP : (part + 1) * VP] for i in range(4)]
                for i in range(3):
                    groups.append(jnp.where(row < NV, four[i], pltpu.roll(four[3], NV - 2 * i, 0)))
            out[slot, part * 96 : (part + 1) * 96] = jnp.concatenate(groups, axis=0).astype(BF16)

    def wait_second(d, carry):
        peer = lax.rem(g + d, 16)
        second(peer, peer).wait_recv()
        return carry

    lax.fori_loop(1, 16, wait_second, 0)
    repack(rho_recv, right_ref, b)

    def copy(buf, slot, part, sems, role, dev):
        where = buf.at[slot] if part is None else buf.at[slot, pl.ds(part * 96, 96)]
        return pltpu.make_async_remote_copy(
            src_ref=where, dst_ref=where, send_sem=sems[0].at[role], recv_sem=sems[1].at[role],
            device_id=dev, device_id_type=MESH,
        )

    started = []

    def go(*args):
        made = copy(*args)
        made.start()
        started.append(made)

    csem = (cs, cr)

    def dev_b(dx, dz):
        return (band_of(bx + dx, bz + dz), g)

    def send_x(n, dz):
        slot = band_of(bx, bz + dz)
        go(right_ref, slot, None, csem, 4 + 4 * n, dev_b(1, 0))
        go(right_ref, slot, None, csem, 5 + 4 * n, dev_b(-1, 0))

    def wait_c(slot, part, role):
        copy(right_ref, slot, part, csem, role, dev_b(1, 0)).wait_recv()

    go(right_ref, b, None, csem, 0, dev_b(0, 1))
    go(right_ref, b, None, csem, 1, dev_b(0, -1))
    send_x(0, 0)

    def wait_third(d, carry):
        peer = lax.rem(g + d, 16)

        @pl.when(jnp.logical_or(b != g, d != 0))
        def _():
            third(peer, peer).wait_recv()

        return carry

    lax.fori_loop(0, 16, wait_third, 0)
    repack(scl_recv, left_ref, g)

    rsem = (rs, rr)

    def dev_g(dl, dy, dc):
        l = gl if dl == 0 else 1 - gl
        c = gc if dc == 0 else 1 - gc
        return (b, ga_of(l, gy + dy, c))

    def slot_g(n, dy, dc):
        return dev_g(n, dy, dc)[1]

    def send_y(n):
        slot = slot_g(n, 0, 0)
        go(left_ref, slot, None, rsem, 1 + 4 * n, dev_g(0, 1, 0))
        go(left_ref, slot, None, rsem, 2 + 4 * n, dev_g(0, -1, 0))

    def send_core(k, n, dy):
        go(left_ref, slot_g(n, dy, 0), None, rsem, 9 + k, dev_g(0, 0, 1))

    def wait_r(slot, part, role):
        copy(left_ref, slot, part, rsem, role, dev_g(0, 1, 0)).wait_recv()

    go(left_ref, g, None, rsem, 0, dev_g(1, 0, 0))
    send_y(0)
    send_core(0, 0, 0)

    wait_c(band_of(bx, bz - 1), None, 0)
    go(right_ref, band_of(bx, bz - 1), 0, csem, 2, dev_b(0, 1))
    send_x(1, -1)
    wait_c(band_of(bx, bz + 1), None, 1)
    go(right_ref, band_of(bx, bz + 1), 1, csem, 3, dev_b(0, -1))
    send_x(2, 1)

    wait_r(slot_g(1, 0, 0), None, 0)
    send_y(1)
    send_core(1, 1, 0)

    def relay_x(n, dz):
        wait_c(band_of(bx - 1, bz + dz), None, 4 + 4 * n)
        go(right_ref, band_of(bx - 1, bz + dz), 0, csem, 6 + 4 * n, dev_b(1, 0))
        wait_c(band_of(bx + 1, bz + dz), None, 5 + 4 * n)
        go(right_ref, band_of(bx + 1, bz + dz), 1, csem, 7 + 4 * n, dev_b(-1, 0))

    def relay_y(n):
        wait_r(slot_g(n, -1, 0), None, 1 + 4 * n)
        go(left_ref, slot_g(n, -1, 0), 0, rsem, 3 + 4 * n, dev_g(0, 1, 0))
        send_core(2 + 3 * n, n, -1)
        wait_r(slot_g(n, 1, 0), None, 2 + 4 * n)
        go(left_ref, slot_g(n, 1, 0), 1, rsem, 4 + 4 * n, dev_g(0, -1, 0))
        send_core(3 + 3 * n, n, 1)

    relay_x(0, 0)
    wait_c(band_of(bx, bz + 2), 0, 2)
    wait_c(band_of(bx, bz + 2), 1, 3)
    send_x(3, 2)
    relay_y(0)
    relay_x(1, -1)
    relay_y(1)
    for n in range(2):
        wait_r(slot_g(n, 2, 0), 0, 3 + 4 * n)
        wait_r(slot_g(n, 2, 0), 1, 4 + 4 * n)
        send_core(4 + 3 * n, n, 2)
    relay_x(2, 1)
    relay_x(3, 2)
    for n, dz in enumerate((0, -1, 1, 2)):
        wait_c(band_of(bx + 2, bz + dz), 0, 6 + 4 * n)
        wait_c(band_of(bx + 2, bz + dz), 1, 7 + 4 * n)
    for k, (n, dy) in enumerate(((0, 0), (1, 0), (0, -1), (0, 1), (0, 2), (1, -1), (1, 1), (1, 2))):
        wait_r(slot_g(n, dy, 1), None, 9 + k)

    for made in started:
        made.wait_send()

    def drain(d, carry):
        dest = lax.rem(g + d, 16)
        first(dest, g).wait_send()
        second(dest, g).wait_send()
        return carry

    lax.fori_loop(1, 16, drain, 0)

    def drain_third(d, carry):
        dest = lax.rem(b + d, 16)

        @pl.when(jnp.logical_or(b != g, d != 0))
        def _():
            third(dest, g).wait_send()

        return carry

    lax.fori_loop(0, 16, drain_third, 0)


def chi_kernel(left_ref, right_ref, out_ref, turned):
    for k in range(16):
        block = right_ref[k]
        turned[k, :96] = -block[96:]
        turned[k, 96:] = block[:96]
    left = left_ref[...].reshape(3072, 256)
    dims = (((0,), (0,)), ((), ()))
    out_ref[:, 0, :] = lax.dot_general(left, right_ref[...].reshape(3072, 256), dims, preferred_element_type=F32)
    out_ref[:, 1, :] = lax.dot_general(left, turned[...].reshape(3072, 256), dims, preferred_element_type=F32)


def body(
    valence_waves,
    conduction_waves,
    valence_energy,
    conduction_energy,
    valence_occupied,
    conduction_occupied,
    gvec_index,
):
    g = lax.axis_index("ga")
    bands = conduction_waves.shape[1]
    factor = float(NV * bands * lax.axis_size("band")) ** (-0.5)
    energy = lax.dynamic_index_in_dim(conduction_energy, g, 0, False)
    occupied = lax.dynamic_index_in_dim(conduction_occupied, g, 0, False)
    weight = (valence_occupied - occupied).astype(F32) / (valence_energy - energy) * factor
    weight = jnp.broadcast_to(jnp.pad(weight, (0, VP - NV))[:, None], (VP, 128))
    valence = jnp.pad(valence_waves.transpose(0, 2, 1, 3), ((0, 0), (0, 0), (0, VP - NV), (0, 0)))
    valence = valence.reshape(2, 2 * VP, 1024)
    conduction = conduction_waves.reshape(2, 2 * bands, 1024)
    gvec = jnp.broadcast_to(gvec_index.reshape(16, 1, 256), (16, VP, 256))
    vmem = pl.BlockSpec(memory_space=pltpu.VMEM)
    dma = pltpu.SemaphoreType.DMA
    left, right = pl.pallas_call(
        kernel,
        out_shape=[jax.ShapeDtypeStruct((16, 192, 256), BF16)] * 2,
        in_specs=[vmem, vmem, pl.BlockSpec(memory_space=pl.ANY), vmem, vmem, vmem, vmem],
        out_specs=[vmem, vmem],
        scratch_shapes=[
            pltpu.VMEM((512, 1024), BF16),
            pltpu.VMEM((512, 1024), BF16),
            pltpu.VMEM((2, 1024, 640), BF16),
            pltpu.VMEM((16, 16, 640), F32),
            pltpu.VMEM((16, 16, 640), F32),
            pltpu.VMEM((16, MAIN + 2 * REST, 256), BF16),
            pltpu.VMEM((16, 16, 256), BF16),
            pltpu.VMEM((16, 16, 256), BF16),
            pltpu.VMEM((16, 16, 256), BF16),
            pltpu.VMEM((16, 16, 256), BF16),
            dma,
            dma((16,)),
            dma((16,)),
            dma((16,)),
            dma((16,)),
            dma((16,)),
            dma((16,)),
            dma((20,)),
            dma((20,)),
            dma((17,)),
            dma((17,)),
        ],
        compiler_params=pltpu.CompilerParams(
            collective_id=0, has_side_effects=True, vmem_limit_bytes=48 * 1024 * 1024
        ),
        name="pairs",
    )(valence, conduction, jnp.asarray(PLANE), jnp.asarray(LINE), jnp.asarray(IDS), gvec, weight)
    return pl.pallas_call(
        chi_kernel,
        out_shape=jax.ShapeDtypeStruct((256, 2, 256), F32),
        in_specs=[vmem, vmem],
        out_specs=vmem,
        scratch_shapes=[pltpu.VMEM((16, 192, 256), BF16)],
        compiler_params=pltpu.CompilerParams(vmem_limit_bytes=48 * 1024 * 1024),
        name="chi",
    )(left, right)


def solution(mesh):
    placed = (
        P(None, None, "ga", None),
        P(None, "band", "ga", None),
        P(),
        P("band"),
        P(),
        P("band"),
        P(),
    )
    return jax.shard_map(
        body, mesh=mesh, in_specs=placed, out_specs=P("band", None, "ga"), check_vma=False
    )
```

```python
import functools

import numpy as np
import jax
import jax.numpy as jnp
import ml_dtypes
from jax import lax
from jax.experimental import pallas as pl
from jax.experimental.pallas import tpu as pltpu
from jax.sharding import PartitionSpec as P

NR = 32
NG = 4096
NV = 6
VP = 8
MAIN = 256
REST = 64
MESH = pl.DeviceIdType.MESH
F32 = jnp.float32
BF16 = jnp.bfloat16


def signed(k):
    return np.where(k > NR // 2, k - NR, k)


def sphere():
    flat = np.arange(NR**3)
    comps = [signed(c) for c in (flat // NR**2, flat // NR % NR, flat % NR)]
    length = sum(c * c for c in comps)
    inside = flat[length <= np.sort(length)[NG - 1]]
    return np.unique(inside // NR**2), np.unique(inside % NR**2)


KX, COLS = sphere()
NK = len(KX)
NC = len(COLS)
assert MAIN < NC <= MAIN + REST
ROWS = 2 * NK * VP


def split(table):
    high = table.astype(ml_dtypes.bfloat16)
    low = (table - high.astype(np.float64)).astype(ml_dtypes.bfloat16)
    return np.stack([high, low])


def plane_table():
    yz = np.arange(NR * NR)
    turns = (yz // NR)[:, None] * (COLS // NR)[None] + (yz % NR)[:, None] * (COLS % NR)[None]
    angle = 2.0 * np.pi / NR * (turns % NR)
    table = np.zeros((NR * NR, 2 * (MAIN + REST)))
    for part, values in enumerate((np.cos(angle), np.sin(angle))):
        table[:, part * MAIN : (part + 1) * MAIN] = values[:, :MAIN]
        start = 2 * MAIN + part * REST
        table[:, start : start + NC - MAIN] = values[:, MAIN:]
    return split(table)


def line_table():
    angle = 2.0 * np.pi / NR * (KX[:, None] * np.arange(NR)[None] % NR)
    norm = float(NR) ** -1.5
    same = np.diag(np.arange(VP) < NV)
    return split(np.concatenate([np.kron(np.cos(angle), same), np.kron(np.sin(angle), same)]) * norm)


def column_ids():
    ids = np.full((MAIN + 2 * REST,), -1, np.int32)
    ids[:NC] = COLS
    return np.ascontiguousarray(np.broadcast_to(ids[:, None], (MAIN + 2 * REST, 128)))


PLANE = plane_table()
LINE = line_table()
IDS = column_ids()


def halves(value):
    high = value.astype(BF16)
    return high, (value - high.astype(F32)).astype(BF16)


def mm(left, right):
    return jnp.dot(left, right, preferred_element_type=F32)


def kernel(
    val_hbm, cond_hbm, plane_hbm, line_hbm, ids_hbm, gvec_hbm, ve_hbm, ce_hbm, vo_hbm, co_hbm,
    out_ref,
    val_ref, cond_ref, table, line_ref, ids_ref, gvec_ref, ve_ref, ce_ref, vo_ref, co_ref,
    left_ref, right_ref, total, pair_hi, pair_lo, a_send, a_recv, hot, rho_send, scl_send, rho_recv, scl_recv,
    in_sem, s1, r1, s2, r2, s3, r3, cs, cr, rs, rr,
):
    b = lax.axis_index("band")
    g = lax.axis_index("ga")
    bx, bz = b // 4, b % 4
    gl, gy, gc = g // 8, g // 2 % 4, g % 2

    def band_of(x, z):
        return lax.rem(x + 4, 4) * 4 + lax.rem(z + 4, 4)

    def ga_of(l, y, c):
        return l * 8 + lax.rem(y + 4, 4) * 2 + c

    inputs = [
        pltpu.make_async_copy(src, dst, in_sem.at[i])
        for i, (src, dst) in enumerate(
            (
                (val_hbm, val_ref),
                (cond_hbm, cond_ref),
                (plane_hbm.at[0], table.at[0]),
                (plane_hbm.at[1], table.at[1]),
                (ids_hbm, ids_ref),
                (gvec_hbm, gvec_ref),
                (line_hbm, line_ref),
                (ve_hbm, ve_ref),
                (ce_hbm, ce_ref),
                (vo_hbm, vo_ref),
                (co_hbm, co_ref),
            )
        )
    ]
    for made in inputs:
        made.start()

    barrier = pltpu.get_barrier_semaphore()
    own = (b == g).astype(jnp.int32)

    def greet(dev):
        pl.semaphore_signal(barrier, inc=1, device_id=dev, device_id_type=MESH)

    def greet_group(d, carry):
        greet((b, lax.rem(g + d, 16)))
        return carry

    lax.fori_loop(1, 16, greet_group, 0)

    def greet_rows(d, carry):
        @pl.when(jnp.logical_or(b != g, d != g))
        def _():
            greet((g, d))

        return carry

    lax.fori_loop(0, 16, greet_rows, 0)
    for dx, dz in ((1, 0), (-1, 0), (0, 1), (0, -1)):
        greet((band_of(bx + dx, bz + dz), g))

    inputs[0].wait()
    inputs[1].wait()
    row8 = lax.broadcasted_iota(jnp.int32, (VP, 1), 0)

    def valence(part, plane):
        out = jnp.zeros((VP, 1024), F32)
        for v in range(NV):
            out = jnp.where(row8 == v, val_ref[part, v].astype(F32)[plane : plane + 1], out)
        return out

    bra = [[valence(part, plane) for plane in range(2)] for part in range(2)]
    for d in range(16):
        c = lax.rem(g + 1 + d, 16)
        cre = cond_ref[0, c].astype(F32)
        cim = cond_ref[1, c].astype(F32)
        parts_re = []
        parts_im = []
        for plane in range(2):
            wre = cre[plane : plane + 1]
            wim = cim[plane : plane + 1]
            parts_re.append(bra[0][plane] * wre + bra[1][plane] * wim)
            parts_im.append(bra[0][plane] * wim - bra[1][plane] * wre)
        for part, values in enumerate((parts_re, parts_im)):
            high, low = halves(jnp.concatenate(values, axis=0))
            at = d // 8 * 256 + part * 128 + 16 * (d % 8)
            pair_hi[at : at + 16] = high
            pair_lo[at : at + 16] = low

    lane = lax.broadcasted_iota(jnp.int32, (1, 128), 1)
    sign = jnp.where(lane < REST, 1.0, -1.0).astype(F32)
    row3 = lax.broadcasted_iota(jnp.int32, (16, VP, 128), 1)

    def first(d, slot):
        return pltpu.make_async_remote_copy(
            src_ref=a_send.at[d], dst_ref=a_recv.at[slot], send_sem=s1.at[d], recv_sem=r1.at[slot],
            device_id=(b, lax.rem(g + 1 + d, 16)), device_id_type=MESH,
        )

    def send_first(d, carry):
        first(d, g).start()
        return carry

    for q in range(2):
        high = pair_hi[q * 256 : q * 256 + 256]
        if q == 0:
            inputs[2].wait()
        both = mm(high, table[0]) + mm(pair_lo[q * 256 : q * 256 + 256], table[0])
        if q == 0:
            inputs[3].wait()
        both = both + mm(high, table[1])
        yre, yim = both[:128], both[128:]
        main_re = yre[:, :MAIN] + yim[:, MAIN : 2 * MAIN]
        main_im = yim[:, :MAIN] - yre[:, MAIN : 2 * MAIN]
        rest = pltpu.roll(yim[:, 2 * MAIN :], REST, 1) + sign * yre[:, 2 * MAIN :]
        tiles = [
            t.reshape(16, VP, 128) for t in (main_re[:, :128], main_re[:, 128:], main_im[:, :128], main_im[:, 128:])
        ]
        for i in range(3):
            packed = jnp.where(row3 < NV, tiles[i], pltpu.roll(tiles[3], NV - 2 * i, 1))
            a_send[8 * q : 8 * q + 8, :, i * 128 : (i + 1) * 128] = packed.reshape(8, 16, 128)
        a_send[8 * q : 8 * q + 8, :, 384:] = rest.reshape(8, 16, 128)
        if q == 0:
            pl.semaphore_wait(barrier, 35 - own)
        lax.fori_loop(8 * q, 8 + 7 * q, send_first, 0)
    a_recv[g] = a_send[15]

    inputs[4].wait()
    inputs[5].wait()

    def one_hot(q, carry):
        for h in range(2):
            for i in range(2):
                yz = jnp.bitwise_and(gvec_ref[pl.ds(2 * q + 16 * i + h, 1)], NR * NR - 1)
                hot[h, q, :, i * 128 : (i + 1) * 128] = jnp.where(ids_ref[...] == yz, 1.0, 0.0).astype(BF16)
        return carry

    lax.fori_loop(0, 8, one_hot, 0)
    for made in inputs[6:]:
        made.wait()

    def wait_first(d, carry):
        first(d, lax.rem(g + 1 + d, 16)).wait_recv()
        return carry

    lax.fori_loop(0, 15, wait_first, 0)

    row3 = lax.broadcasted_iota(jnp.int32, (32, VP, 128), 1)
    tiles = [a_recv[:, :, i * 128 : (i + 1) * 128].reshape(32, VP, 128) for i in range(3)]
    last = pltpu.roll(tiles[2], 6, 1)
    for i in (1, 0):
        last = jnp.where(row3 < 2 * i + 2, pltpu.roll(tiles[i], 2 + 2 * i, 1), last)
    whole = [t.reshape(256, 128) for t in (*tiles, last)] + [a_recv[:, :, 384:].reshape(256, 128)]
    a_hi, a_lo = halves(jnp.concatenate(whole, axis=1))
    uv = mm(line_ref[0], a_hi) + mm(line_ref[0], a_lo) + mm(line_ref[1], a_hi)
    u, v = uv[: ROWS // 2], uv[ROWS // 2 :]
    rest = u[:, 2 * MAIN :] + sign * pltpu.roll(v[:, 2 * MAIN :], REST, 1)
    z_re = jnp.concatenate([u[:, :MAIN] + v[:, MAIN : 2 * MAIN], rest], axis=1)
    z_im = jnp.concatenate([u[:, MAIN : 2 * MAIN] - v[:, :MAIN], pltpu.roll(rest, REST, 1)], axis=1)
    z = jnp.concatenate([z_re, z_im], axis=0).astype(BF16)
    level = jnp.zeros((VP, 256), F32)
    filled = jnp.zeros((VP, 256), jnp.int32)
    for v in range(NV):
        level = jnp.where(row8 == v, ve_ref[v], level)
        filled = jnp.where(row8 == v, vo_ref[v], filled)
    factor = float(NV * 256) ** -0.5
    weight = (filled - co_ref[g]).astype(F32) / (level - ce_ref[g]) * factor

    def second(h, dest, slot):
        return pltpu.make_async_remote_copy(
            src_ref=rho_send.at[h, dest], dst_ref=rho_recv.at[h, slot],
            send_sem=s2.at[h, dest], recv_sem=r2.at[h, slot],
            device_id=(b, dest), device_id_type=MESH,
        )

    def third(h, dest, slot):
        return pltpu.make_async_remote_copy(
            src_ref=scl_send.at[h, dest], dst_ref=scl_recv.at[h, slot],
            send_sem=s3.at[h, dest], recv_sem=r3.at[h, slot],
            device_id=(dest, b), device_id_type=MESH,
        )

    def pick(h, d, carry):
        q = lax.rem(g + d, 8)
        found = mm(z, hot[h, q])
        kx = jnp.concatenate([gvec_ref[pl.ds(2 * q + 16 * i + h, 1)] for i in range(2)], axis=1)
        kx = jnp.broadcast_to(jnp.right_shift(kx, 10), (VP, 256))
        re = jnp.zeros((VP, 256), F32)
        im = jnp.zeros((VP, 256), F32)
        for k in range(NK):
            here = kx == int(KX[k])
            re = jnp.where(here, found[k * VP : (k + 1) * VP], re)
            im = jnp.where(here, found[(NK + k) * VP : (NK + k + 1) * VP], im)
        rho = jnp.concatenate([re, im], axis=0).astype(BF16)
        scaled = jnp.concatenate([re * weight, im * weight], axis=0).astype(BF16)
        for i in range(2):
            j = q + 8 * i
            rho_send[h, j] = rho[:, i * 128 : (i + 1) * 128]
            scl_send[h, j] = scaled[:, i * 128 : (i + 1) * 128]

            @pl.when(j != g)
            def _():
                second(h, j, g).start()

            @pl.when(jnp.logical_or(b != g, j != g))
            def _():
                third(h, j, g).start()

        return carry

    row = lax.broadcasted_iota(jnp.int32, (VP, 128), 0)

    def repack(src, out, h, slot):
        for part in range(2):
            groups = []
            for quad in range(4):
                four = [src[h, 4 * quad + i].astype(F32)[part * VP : (part + 1) * VP] for i in range(4)]
                for i in range(3):
                    groups.append(jnp.where(row < NV, four[i], pltpu.roll(four[3], NV - 2 * i, 0)))
            out[h, slot, part * 96 : (part + 1) * 96] = jnp.concatenate(groups, axis=0).astype(BF16)

    def wait_second(h, d, carry):
        peer = lax.rem(g + d, 16)
        second(h, peer, peer).wait_recv()
        return carry

    def wait_third(h, d, carry):
        peer = lax.rem(g + d, 16)

        @pl.when(jnp.logical_or(b != g, d != 0))
        def _():
            third(h, peer, peer).wait_recv()

        return carry

    started = []

    def copy(buf, h, slot, part, sems, role, dev):
        where = buf.at[h, slot] if part is None else buf.at[h, slot, pl.ds(part * 96, 96)]
        return pltpu.make_async_remote_copy(
            src_ref=where, dst_ref=where, send_sem=sems[0].at[h, role], recv_sem=sems[1].at[h, role],
            device_id=dev, device_id_type=MESH,
        )

    def go(*args):
        made = copy(*args)
        made.start()
        started.append(made)

    csem = (cs, cr)

    def dev_b(dx, dz):
        return (band_of(bx + dx, bz + dz), g)

    def send_x(h, n, dz):
        slot = band_of(bx, bz + dz)
        go(right_ref, h, slot, None, csem, 4 + 4 * n, dev_b(1, 0))
        go(right_ref, h, slot, None, csem, 5 + 4 * n, dev_b(-1, 0))

    def wait_c(h, slot, part, role):
        copy(right_ref, h, slot, part, csem, role, dev_b(1, 0)).wait_recv()

    def relay_x(h, n, dz):
        for part, dx in enumerate((1, -1)):
            slot = band_of(bx - dx, bz + dz)
            wait_c(h, slot, None, 4 + 4 * n + part)
            go(right_ref, h, slot, part, csem, 6 + 4 * n + part, dev_b(dx, 0))

    def relay_z(h):
        for part, dz in enumerate((1, -1)):
            slot = band_of(bx, bz - dz)
            wait_c(h, slot, None, part)
            go(right_ref, h, slot, part, csem, 2 + part, dev_b(0, dz))
            send_x(h, 1 + part, -dz)

    def far_z(h):
        wait_c(h, band_of(bx, bz + 2), 0, 2)
        wait_c(h, band_of(bx, bz + 2), 1, 3)
        send_x(h, 3, 2)

    rsem = (rs, rr)

    def dev_g(dl, dy, dc):
        return (b, ga_of(1 - gl if dl else gl, gy + dy, 1 - gc if dc else gc))

    def send_y(h, n):
        slot = dev_g(n, 0, 0)[1]
        for i, dy in enumerate((1, -1, 2)):
            go(left_ref, h, slot, None, rsem, 1 + 3 * n + i, dev_g(0, dy, 0))

    def wait_r(h, slot, role):
        copy(left_ref, h, slot, None, rsem, role, dev_g(0, 1, 0)).wait_recv()

    def send_core(h, n, k):
        go(left_ref, h, dev_g(n, (0, -1, 1, 2)[k], 0)[1], None, rsem, 7 + 4 * n + k, dev_g(0, 0, 1))

    def relay_l(h):
        wait_r(h, dev_g(1, 0, 0)[1], 0)
        send_y(h, 1)
        send_core(h, 1, 0)

    def relay_y(h, n):
        for k, dy in enumerate((-1, 1, 2)):
            wait_r(h, dev_g(n, dy, 0)[1], 1 + 3 * n + k)
            send_core(h, n, k + 1)

    for h in range(2):
        lax.fori_loop(1, 9, functools.partial(pick, h), 0)
        rho_recv[h, g] = rho_send[h, g]

        @pl.when(b == g)
        def _():
            scl_recv[h, g] = scl_send[h, g]

    for h in range(2):
        lax.fori_loop(1, 16, functools.partial(wait_second, h), 0)
        repack(rho_recv, right_ref, h, b)
        go(right_ref, h, b, None, csem, 0, dev_b(0, 1))
        go(right_ref, h, b, None, csem, 1, dev_b(0, -1))
        send_x(h, 0, 0)
        lax.fori_loop(0, 16, functools.partial(wait_third, h), 0)
        repack(scl_recv, left_ref, h, g)
        go(left_ref, h, g, None, rsem, 0, dev_g(1, 0, 0))
        send_y(h, 0)
        send_core(h, 0, 0)

    for h in range(2):
        relay_l(h)
        relay_x(h, 0, 0)
        relay_z(h)
    relay_y(0, 0)
    relay_x(0, 1, -1)
    relay_x(0, 2, 1)
    far_z(0)
    relay_y(1, 0)
    relay_y(0, 1)
    relay_x(1, 1, -1)
    relay_x(1, 2, 1)
    far_z(1)
    relay_y(1, 1)
    relay_x(0, 3, 2)
    relay_x(1, 3, 2)
    for h in range(2):
        for n in range(2):
            for k, dy in enumerate((0, -1, 1, 2)):
                wait_r(h, dev_g(n, dy, 1)[1], 7 + 4 * n + k)

    dims = (((0,), (0,)), ((), ()))
    for n, dz in enumerate((0, -1, 1, 2)):
        for h in range(2):
            for part in range(2):
                wait_c(h, band_of(bx + 2, bz + dz), part, 6 + 4 * n + part)
        slots = [band_of(x, bz + dz) for x in range(4)]
        left = jnp.concatenate([jnp.concatenate([left_ref[h, k] for k in slots], axis=0) for h in range(2)], axis=1)
        right = jnp.concatenate([jnp.concatenate([right_ref[h, k] for k in slots], axis=0) for h in range(2)], axis=1)
        turned = jnp.concatenate(
            [t for k in range(4) for t in (-right[192 * k + 96 : 192 * k + 192], right[192 * k : 192 * k + 96])], axis=0
        )
        for part, other in enumerate((right, turned)):
            value = lax.dot_general(left, other, dims, preferred_element_type=F32)
            if n == 0:
                total[part] = value
            elif n < 3:
                total[part] += value
            else:
                out_ref[:, part, :] = total[part] + value

    for made in started:
        made.wait_send()

    def drain(d, carry):
        first(d - 1, g).wait_send()
        for h in range(2):
            second(h, lax.rem(g + d, 16), g).wait_send()
        return carry

    lax.fori_loop(1, 16, drain, 0)

    def drain_third(d, carry):
        dest = lax.rem(b + d, 16)

        @pl.when(jnp.logical_or(b != g, d != 0))
        def _():
            for h in range(2):
                third(h, dest, g).wait_send()

        return carry

    lax.fori_loop(0, 16, drain_third, 0)


def body(
    valence_waves,
    conduction_waves,
    valence_energy,
    conduction_energy,
    valence_occupied,
    conduction_occupied,
    gvec_index,
):
    vmem = pl.BlockSpec(memory_space=pltpu.VMEM)
    hbm = pl.BlockSpec(memory_space=pltpu.HBM)
    dma = pltpu.SemaphoreType.DMA
    return pl.pallas_call(
        kernel,
        out_shape=jax.ShapeDtypeStruct((256, 2, 256), F32),
        in_specs=[hbm] * 10,
        out_specs=vmem,
        scratch_shapes=[
            pltpu.VMEM(valence_waves.shape, BF16),
            pltpu.VMEM(conduction_waves.shape, BF16),
            pltpu.VMEM(PLANE.shape, BF16),
            pltpu.VMEM(LINE.shape, BF16),
            pltpu.VMEM(IDS.shape, jnp.int32),
            pltpu.VMEM((32, 128), jnp.int32),
            pltpu.SMEM((NV,), F32),
            pltpu.SMEM((16,), F32),
            pltpu.SMEM((NV,), jnp.int32),
            pltpu.SMEM((16,), jnp.int32),
            pltpu.VMEM((2, 16, 192, 128), BF16),
            pltpu.VMEM((2, 16, 192, 128), BF16),
            pltpu.VMEM((2, 256, 256), F32),
            pltpu.VMEM((512, 1024), BF16),
            pltpu.VMEM((512, 1024), BF16),
            pltpu.VMEM((16, 16, 512), F32),
            pltpu.VMEM((16, 16, 512), F32),
            pltpu.VMEM((2, 8, MAIN + 2 * REST, 256), BF16),
            pltpu.VMEM((2, 16, 16, 128), BF16),
            pltpu.VMEM((2, 16, 16, 128), BF16),
            pltpu.VMEM((2, 16, 16, 128), BF16),
            pltpu.VMEM((2, 16, 16, 128), BF16),
            dma((11,)),
            dma((16,)),
            dma((16,)),
            dma((2, 16)),
            dma((2, 16)),
            dma((2, 16)),
            dma((2, 16)),
            dma((2, 20)),
            dma((2, 20)),
            dma((2, 15)),
            dma((2, 15)),
        ],
        compiler_params=pltpu.CompilerParams(
            collective_id=0, has_side_effects=True, vmem_limit_bytes=60 * 1024 * 1024
        ),
        name="pairs",
    )(
        valence_waves, conduction_waves, jnp.asarray(PLANE), jnp.asarray(LINE), jnp.asarray(IDS),
        gvec_index.reshape(32, 128), valence_energy, conduction_energy, valence_occupied, conduction_occupied,
    )


def solution(mesh):
    placed = (
        P(None, None, "ga", None),
        P(None, "band", "ga", None),
        P(),
        P("band"),
        P(),
        P("band"),
        P(),
    )
    return jax.shard_map(
        body, mesh=mesh, in_specs=placed, out_specs=P("band", None, "ga"), check_vma=False
    )
```

```python
import functools

import numpy as np
import jax
import jax.numpy as jnp
import ml_dtypes
from jax import lax
from jax.experimental import pallas as pl
from jax.experimental.pallas import tpu as pltpu
from jax.sharding import PartitionSpec as P

NR = 32
NG = 4096
NV = 6
VP = 8
MAIN = 256
REST = 64
MESH = pl.DeviceIdType.MESH
F32 = jnp.float32
BF16 = jnp.bfloat16


def signed(k):
    return np.where(k > NR // 2, k - NR, k)


def sphere():
    flat = np.arange(NR**3)
    comps = [signed(c) for c in (flat // NR**2, flat // NR % NR, flat % NR)]
    length = sum(c * c for c in comps)
    inside = flat[length <= np.sort(length)[NG - 1]]
    return np.unique(inside // NR**2), np.unique(inside % NR**2)


KX, COLS = sphere()


def mirrored(cols):
    return (-(cols // NR) % NR) * NR + -(cols % NR) % NR


PLUS = COLS[COLS < mirrored(COLS)][: MAIN // 2]
OTHER = np.setdiff1d(COLS, np.concatenate([PLUS, mirrored(PLUS)]))
COLS = np.concatenate([PLUS, mirrored(PLUS), OTHER])
NK = len(KX)
NC = len(COLS)
assert len(PLUS) == MAIN // 2 and len(OTHER) <= REST
ROWS = 2 * NK * VP


def split(table):
    high = table.astype(ml_dtypes.bfloat16)
    low = (table - high.astype(np.float64)).astype(ml_dtypes.bfloat16)
    return np.stack([high, low])


def plane_table():
    yz = np.arange(NR * NR)
    table = np.zeros((NR * NR, MAIN + 2 * REST))
    for cols, start, step in ((PLUS, 0, MAIN // 2), (OTHER, MAIN, REST)):
        turns = (yz // NR)[:, None] * (cols // NR)[None] + (yz % NR)[:, None] * (cols % NR)[None]
        angle = 2.0 * np.pi / NR * (turns % NR)
        table[:, start : start + len(cols)] = np.cos(angle)
        table[:, start + step : start + step + len(cols)] = np.sin(angle)
    return split(table)


def line_table():
    angle = 2.0 * np.pi / NR * (KX[:, None] * np.arange(NR)[None] % NR)
    norm = float(NR) ** -1.5
    same = np.diag(np.arange(VP) < NV)
    return split(np.concatenate([np.kron(np.cos(angle), same), np.kron(np.sin(angle), same)]) * norm)


def column_ids():
    ids = np.full((MAIN + 2 * REST,), -1, np.int32)
    ids[:NC] = COLS
    return np.ascontiguousarray(np.broadcast_to(ids[:, None], (MAIN + 2 * REST, 128)))


PLANE = plane_table()
LINE = line_table()
IDS = column_ids()


def halves(value):
    high = value.astype(BF16)
    return high, (value - high.astype(F32)).astype(BF16)


def mm(left, right):
    return jnp.dot(left, right, preferred_element_type=F32)


def kernel(
    val_hbm, cond_hbm, plane_hbm, line_hbm, ids_hbm, gvec_hbm, ve_hbm, ce_hbm, vo_hbm, co_hbm,
    out_ref,
    val_ref, cond_ref, table, line_ref, ids_ref, gvec_ref, ve_ref, ce_ref, vo_ref, co_ref,
    left_ref, right_ref, total, pair_hi, pair_lo, a_send, a_recv, hot, rho_send, scl_send, rho_recv, scl_recv,
    hear, in_sem, s1, r1, s2, r2, s3, r3, cs, cr, rs, rr,
):
    b = lax.axis_index("band")
    g = lax.axis_index("ga")
    bx, bz = b // 4, b % 4
    gl, gy, gc = g // 8, g // 2 % 4, g % 2

    def band_of(x, z):
        return lax.rem(x + 4, 4) * 4 + lax.rem(z + 4, 4)

    def ga_of(l, y, c):
        return l * 8 + lax.rem(y + 4, 4) * 2 + c

    inputs = [
        pltpu.make_async_copy(src, dst, in_sem.at[i])
        for i, (src, dst) in enumerate(
            (
                (val_hbm, val_ref),
                (cond_hbm, cond_ref),
                (plane_hbm.at[0], table.at[0]),
                (plane_hbm.at[1], table.at[1]),
                (ids_hbm, ids_ref),
                (gvec_hbm, gvec_ref),
                (line_hbm, line_ref),
                (ve_hbm, ve_ref),
                (ce_hbm, ce_ref),
                (vo_hbm, vo_ref),
                (co_hbm, co_ref),
            )
        )
    ]
    for made in inputs:
        made.start()

    barrier = pltpu.get_barrier_semaphore()

    def greet(dev):
        pl.semaphore_signal(barrier, inc=1, device_id=dev, device_id_type=MESH)

    def greet_group(d, carry):
        greet((b, lax.rem(g + d, 16)))
        return carry

    lax.fori_loop(1, 16, greet_group, 0)

    for dx, dz in ((1, 0), (-1, 0), (0, 1), (0, -1)):
        greet((band_of(bx + dx, bz + dz), g))

    def tell(step):
        for way in (1, -1):
            dev = (band_of(bx + way, bz), g) if step < 2 else (band_of(bx, bz + way), g)
            pl.semaphore_signal(hear.at[step], inc=1, device_id=dev, device_id_type=MESH)

    def heard(step):
        pl.semaphore_wait(hear.at[step], 2)

    inputs[0].wait()
    inputs[1].wait()
    row8 = lax.broadcasted_iota(jnp.int32, (VP, 1), 0)

    def valence(part, plane):
        out = jnp.zeros((VP, 1024), F32)
        for v in range(NV):
            out = jnp.where(row8 == v, val_ref[part, v].astype(F32)[plane : plane + 1], out)
        return out

    bra = [[valence(part, plane) for plane in range(2)] for part in range(2)]
    for d in range(16):
        c = lax.rem(g + 1 + d, 16)
        cre = cond_ref[0, c].astype(F32)
        cim = cond_ref[1, c].astype(F32)
        parts_re = []
        parts_im = []
        for plane in range(2):
            wre = cre[plane : plane + 1]
            wim = cim[plane : plane + 1]
            parts_re.append(bra[0][plane] * wre + bra[1][plane] * wim)
            parts_im.append(bra[0][plane] * wim - bra[1][plane] * wre)
        for part, values in enumerate((parts_re, parts_im)):
            high, low = halves(jnp.concatenate(values, axis=0))
            at = d // 8 * 256 + part * 128 + 16 * (d % 8)
            pair_hi[at : at + 16] = high
            pair_lo[at : at + 16] = low

    lane = lax.broadcasted_iota(jnp.int32, (1, 128), 1)
    sign = jnp.where(lane < REST, 1.0, -1.0).astype(F32)
    row3 = lax.broadcasted_iota(jnp.int32, (16, VP, 128), 1)

    def first(d, slot):
        return pltpu.make_async_remote_copy(
            src_ref=a_send.at[d], dst_ref=a_recv.at[slot], send_sem=s1.at[d], recv_sem=r1.at[slot],
            device_id=(b, lax.rem(g + 1 + d, 16)), device_id_type=MESH,
        )

    def send_first(d, carry):
        first(d, g).start()
        return carry

    for q in range(2):
        high = pair_hi[q * 256 : q * 256 + 256]
        if q == 0:
            inputs[2].wait()
        both = mm(high, table[0]) + mm(pair_lo[q * 256 : q * 256 + 256], table[0])
        if q == 0:
            inputs[3].wait()
        both = both + mm(high, table[1])
        yre, yim = both[:128], both[128:]
        cre, sre, cim, sim = (t[:, i * 128 : (i + 1) * 128] for t in (yre, yim) for i in range(2))
        rest = pltpu.roll(yim[:, MAIN:], REST, 1) + sign * yre[:, MAIN:]
        tiles = [t.reshape(16, VP, 128) for t in (cre + sim, cre - sim, cim - sre, cim + sre)]
        for i in range(3):
            packed = jnp.where(row3 < NV, tiles[i], pltpu.roll(tiles[3], NV - 2 * i, 1))
            a_send[8 * q : 8 * q + 8, :, i * 128 : (i + 1) * 128] = packed.reshape(8, 16, 128)
        a_send[8 * q : 8 * q + 8, :, 384:] = rest.reshape(8, 16, 128)
        if q == 0:
            pl.semaphore_wait(barrier, 19)
        lax.fori_loop(8 * q, 8 + 7 * q, send_first, 0)
        if q == 1:
            heard(0)
        tell(q)
    a_recv[g] = a_send[15]

    inputs[4].wait()
    inputs[5].wait()

    def one_hot(q, carry):
        for h in range(2):
            for i in range(2):
                yz = jnp.bitwise_and(gvec_ref[pl.ds(2 * q + 16 * i + h, 1)], NR * NR - 1)
                hot[h, q, :, i * 128 : (i + 1) * 128] = jnp.where(ids_ref[...] == yz, 1.0, 0.0).astype(BF16)
        return carry

    lax.fori_loop(0, 8, one_hot, 0)
    heard(1)
    tell(2)
    for made in inputs[6:]:
        made.wait()

    def wait_first(d, carry):
        first(d, lax.rem(g + 1 + d, 16)).wait_recv()
        return carry

    lax.fori_loop(0, 15, wait_first, 0)
    heard(2)
    tell(3)

    row3 = lax.broadcasted_iota(jnp.int32, (32, VP, 128), 1)
    tiles = [a_recv[:, :, i * 128 : (i + 1) * 128].reshape(32, VP, 128) for i in range(3)]
    last = pltpu.roll(tiles[2], 6, 1)
    for i in (1, 0):
        last = jnp.where(row3 < 2 * i + 2, pltpu.roll(tiles[i], 2 + 2 * i, 1), last)
    whole = [t.reshape(256, 128) for t in (*tiles, last)] + [a_recv[:, :, 384:].reshape(256, 128)]
    a_hi, a_lo = halves(jnp.concatenate(whole, axis=1))
    uv = mm(line_ref[0], a_hi) + mm(line_ref[0], a_lo) + mm(line_ref[1], a_hi)
    u, v = uv[: ROWS // 2], uv[ROWS // 2 :]
    rest = u[:, 2 * MAIN :] + sign * pltpu.roll(v[:, 2 * MAIN :], REST, 1)
    z_re = jnp.concatenate([u[:, :MAIN] + v[:, MAIN : 2 * MAIN], rest], axis=1)
    z_im = jnp.concatenate([u[:, MAIN : 2 * MAIN] - v[:, :MAIN], pltpu.roll(rest, REST, 1)], axis=1)
    z = jnp.concatenate([z_re, z_im], axis=0).astype(BF16)
    level = jnp.zeros((VP, 256), F32)
    filled = jnp.zeros((VP, 256), jnp.int32)
    for v in range(NV):
        level = jnp.where(row8 == v, ve_ref[v], level)
        filled = jnp.where(row8 == v, vo_ref[v], filled)
    factor = float(NV * 256) ** -0.5
    weight = (filled - co_ref[g]).astype(F32) / (level - ce_ref[g]) * factor

    def second(h, dest, slot):
        return pltpu.make_async_remote_copy(
            src_ref=rho_send.at[h, dest], dst_ref=rho_recv.at[h, slot],
            send_sem=s2.at[h, dest], recv_sem=r2.at[h, slot],
            device_id=(b, dest), device_id_type=MESH,
        )

    def third(h, dest, slot):
        return pltpu.make_async_remote_copy(
            src_ref=scl_send.at[h, dest], dst_ref=scl_recv.at[h, slot],
            send_sem=s3.at[h, dest], recv_sem=r3.at[h, slot],
            device_id=(dest, b), device_id_type=MESH,
        )

    def pick(h, d):
        q = lax.rem(g + d, 8)
        found = mm(z, hot[h, q])
        kx = jnp.concatenate([gvec_ref[pl.ds(2 * q + 16 * i + h, 1)] for i in range(2)], axis=1)
        kx = jnp.broadcast_to(jnp.right_shift(kx, 10), (VP, 256))
        re = jnp.zeros((VP, 256), F32)
        im = jnp.zeros((VP, 256), F32)
        for k in range(NK):
            here = kx == int(KX[k])
            re = jnp.where(here, found[k * VP : (k + 1) * VP], re)
            im = jnp.where(here, found[(NK + k) * VP : (NK + k + 1) * VP], im)
        rho = jnp.concatenate([re, im], axis=0).astype(BF16)
        scaled = jnp.concatenate([re * weight, im * weight], axis=0).astype(BF16)
        for i in range(2):
            rho_send[h, q + 8 * i] = rho[:, i * 128 : (i + 1) * 128]
            scl_send[h, q + 8 * i] = scaled[:, i * 128 : (i + 1) * 128]

    def send_second(h, d, carry):
        second(h, lax.rem(g + d, 16), g).start()
        return carry

    def send_third(h, d, carry):
        third(h, lax.rem(g + d, 16), g).start()
        return carry

    row = lax.broadcasted_iota(jnp.int32, (VP, 128), 0)

    def repack(src, out, h, slot):
        for part in range(2):
            groups = []
            for quad in range(4):
                four = [src[h, 4 * quad + i].astype(F32)[part * VP : (part + 1) * VP] for i in range(4)]
                for i in range(3):
                    groups.append(jnp.where(row < NV, four[i], pltpu.roll(four[3], NV - 2 * i, 0)))
            out[h, slot, part * 96 : (part + 1) * 96] = jnp.concatenate(groups, axis=0).astype(BF16)

    def wait_second(h, d, carry):
        peer = lax.rem(g + d, 16)
        second(h, peer, peer).wait_recv()
        return carry

    def wait_third(h, d, carry):
        peer = lax.rem(g + d, 16)

        @pl.when(jnp.logical_or(b != g, d != 0))
        def _():
            third(h, peer, peer).wait_recv()

        return carry

    started = []

    def copy(buf, h, slot, part, sems, role, dev):
        where = buf.at[h, slot] if part is None else buf.at[h, slot, pl.ds(part * 96, 96)]
        return pltpu.make_async_remote_copy(
            src_ref=where, dst_ref=where, send_sem=sems[0].at[h, role], recv_sem=sems[1].at[h, role],
            device_id=dev, device_id_type=MESH,
        )

    def go(*args):
        made = copy(*args)
        made.start()
        started.append(made)

    csem = (cs, cr)

    def dev_b(dx, dz):
        return (band_of(bx + dx, bz + dz), g)

    def send_x(h, n, dz):
        slot = band_of(bx, bz + dz)
        go(right_ref, h, slot, None, csem, 4 + 4 * n, dev_b(1, 0))
        go(right_ref, h, slot, None, csem, 5 + 4 * n, dev_b(-1, 0))

    def wait_c(h, slot, part, role):
        copy(right_ref, h, slot, part, csem, role, dev_b(1, 0)).wait_recv()

    def relay_x(h, n, dz):
        for part, dx in enumerate((1, -1)):
            slot = band_of(bx - dx, bz + dz)
            wait_c(h, slot, None, 4 + 4 * n + part)
            go(right_ref, h, slot, part, csem, 6 + 4 * n + part, dev_b(dx, 0))

    def relay_z(h):
        for part, dz in enumerate((1, -1)):
            slot = band_of(bx, bz - dz)
            wait_c(h, slot, None, part)
            go(right_ref, h, slot, part, csem, 2 + part, dev_b(0, dz))
            send_x(h, 1 + part, -dz)

    def far_z(h):
        wait_c(h, band_of(bx, bz + 2), 0, 2)
        wait_c(h, band_of(bx, bz + 2), 1, 3)
        send_x(h, 3, 2)

    rsem = (rs, rr)

    def dev_g(dl, dy, dc):
        return (b, ga_of(1 - gl if dl else gl, gy + dy, 1 - gc if dc else gc))

    def send_y(h, n):
        slot = dev_g(n, 0, 0)[1]
        for i, dy in enumerate((1, -1, 2)):
            go(left_ref, h, slot, None, rsem, 1 + 3 * n + i, dev_g(0, dy, 0))

    def wait_r(h, slot, role):
        copy(left_ref, h, slot, None, rsem, role, dev_g(0, 1, 0)).wait_recv()

    def send_core(h, n, k):
        go(left_ref, h, dev_g(n, (0, -1, 1, 2)[k], 0)[1], None, rsem, 7 + 4 * n + k, dev_g(0, 0, 1))

    def relay_l(h):
        wait_r(h, dev_g(1, 0, 0)[1], 0)
        send_y(h, 1)
        send_core(h, 1, 0)

    def relay_y(h, n):
        for k, dy in enumerate((-1, 1, 2)):
            wait_r(h, dev_g(n, dy, 0)[1], 1 + 3 * n + k)
            send_core(h, n, k + 1)

    def all_thirds(h):
        lax.fori_loop(1, 16, functools.partial(send_third, h), 0)

        @pl.when(b != g)
        def _():
            third(h, g, g).start()

        @pl.when(b == g)
        def _():
            scl_recv[h, g] = scl_send[h, g]

    for h in range(2):
        for d in range(1, 9):
            pick(h, d)
        lax.fori_loop(1, 16, functools.partial(send_second, h), 0)
        rho_recv[h, g] = rho_send[h, g]
    heard(3)
    all_thirds(0)
    all_thirds(1)

    def rows(h):
        lax.fori_loop(0, 16, functools.partial(wait_third, h), 0)
        repack(scl_recv, left_ref, h, g)
        go(left_ref, h, g, None, rsem, 0, dev_g(1, 0, 0))
        send_y(h, 0)
        send_core(h, 0, 0)

    for h in range(2):
        lax.fori_loop(1, 16, functools.partial(wait_second, h), 0)
        repack(rho_recv, right_ref, h, b)
        go(right_ref, h, b, None, csem, 0, dev_b(0, 1))
        go(right_ref, h, b, None, csem, 1, dev_b(0, -1))
        send_x(h, 0, 0)
    for h in range(2):
        relay_x(h, 0, 0)
        rows(h)
        relay_z(h)
    relay_l(0)
    relay_l(1)
    for h in range(2):
        relay_x(h, 1, -1)
        relay_x(h, 2, 1)
        far_z(h)
        relay_y(h, 0)
    for h in range(2):
        relay_y(h, 1)
        relay_x(h, 3, 2)
    for h in range(2):
        for n in range(2):
            for k, dy in enumerate((0, -1, 1, 2)):
                wait_r(h, dev_g(n, dy, 1)[1], 7 + 4 * n + k)

    dims = (((0,), (0,)), ((), ()))
    for n, dz in enumerate((0, -1, 1, 2)):
        for h in range(2):
            for part in range(2):
                wait_c(h, band_of(bx + 2, bz + dz), part, 6 + 4 * n + part)
        slots = [band_of(x, bz + dz) for x in range(4)]
        left = jnp.concatenate([jnp.concatenate([left_ref[h, k] for k in slots], axis=0) for h in range(2)], axis=1)
        right = jnp.concatenate([jnp.concatenate([right_ref[h, k] for k in slots], axis=0) for h in range(2)], axis=1)
        turned = jnp.concatenate(
            [t for k in range(4) for t in (-right[192 * k + 96 : 192 * k + 192], right[192 * k : 192 * k + 96])], axis=0
        )
        for part, other in enumerate((right, turned)):
            value = lax.dot_general(left, other, dims, preferred_element_type=F32)
            if n == 0:
                total[part] = value
            elif n < 3:
                total[part] += value
            else:
                out_ref[:, part, :] = total[part] + value

    for made in started:
        made.wait_send()

    def drain(d, carry):
        first(d - 1, g).wait_send()
        for h in range(2):
            second(h, lax.rem(g + d, 16), g).wait_send()
        return carry

    lax.fori_loop(1, 16, drain, 0)

    def drain_third(d, carry):
        dest = lax.rem(b + d, 16)

        @pl.when(jnp.logical_or(b != g, d != 0))
        def _():
            for h in range(2):
                third(h, dest, g).wait_send()

        return carry

    lax.fori_loop(0, 16, drain_third, 0)


def body(
    valence_waves,
    conduction_waves,
    valence_energy,
    conduction_energy,
    valence_occupied,
    conduction_occupied,
    gvec_index,
):
    vmem = pl.BlockSpec(memory_space=pltpu.VMEM)
    hbm = pl.BlockSpec(memory_space=pltpu.HBM)
    dma = pltpu.SemaphoreType.DMA
    return pl.pallas_call(
        kernel,
        out_shape=jax.ShapeDtypeStruct((256, 2, 256), F32),
        in_specs=[hbm] * 10,
        out_specs=vmem,
        scratch_shapes=[
            pltpu.VMEM(valence_waves.shape, BF16),
            pltpu.VMEM(conduction_waves.shape, BF16),
            pltpu.VMEM(PLANE.shape, BF16),
            pltpu.VMEM(LINE.shape, BF16),
            pltpu.VMEM(IDS.shape, jnp.int32),
            pltpu.VMEM((32, 128), jnp.int32),
            pltpu.SMEM((NV,), F32),
            pltpu.SMEM((16,), F32),
            pltpu.SMEM((NV,), jnp.int32),
            pltpu.SMEM((16,), jnp.int32),
            pltpu.VMEM((2, 16, 192, 128), BF16),
            pltpu.VMEM((2, 16, 192, 128), BF16),
            pltpu.VMEM((2, 256, 256), F32),
            pltpu.VMEM((512, 1024), BF16),
            pltpu.VMEM((512, 1024), BF16),
            pltpu.VMEM((16, 16, 512), F32),
            pltpu.VMEM((16, 16, 512), F32),
            pltpu.VMEM((2, 8, MAIN + 2 * REST, 256), BF16),
            pltpu.VMEM((2, 16, 16, 128), BF16),
            pltpu.VMEM((2, 16, 16, 128), BF16),
            pltpu.VMEM((2, 16, 16, 128), BF16),
            pltpu.VMEM((2, 16, 16, 128), BF16),
            pltpu.SemaphoreType.REGULAR((4,)),
            dma((11,)),
            dma((16,)),
            dma((16,)),
            dma((2, 16)),
            dma((2, 16)),
            dma((2, 16)),
            dma((2, 16)),
            dma((2, 20)),
            dma((2, 20)),
            dma((2, 15)),
            dma((2, 15)),
        ],
        compiler_params=pltpu.CompilerParams(
            collective_id=0, has_side_effects=True, vmem_limit_bytes=60 * 1024 * 1024
        ),
        name="pairs",
    )(
        valence_waves, conduction_waves, jnp.asarray(PLANE), jnp.asarray(LINE), jnp.asarray(IDS),
        gvec_index.reshape(32, 128), valence_energy, conduction_energy, valence_occupied, conduction_occupied,
    )


def solution(mesh):
    placed = (
        P(None, None, "ga", None),
        P(None, "band", "ga", None),
        P(),
        P("band"),
        P(),
        P("band"),
        P(),
    )
    return jax.shard_map(
        body, mesh=mesh, in_specs=placed, out_specs=P("band", None, "ga"), check_vma=False
    )
```

```python
import functools

import numpy as np
import jax
import jax.numpy as jnp
import ml_dtypes
from jax import lax
from jax.experimental import pallas as pl
from jax.experimental.pallas import tpu as pltpu
from jax.sharding import PartitionSpec as P

NR = 32
NG = 4096
NV = 6
VP = 8
MAIN = 256
REST = 64
STRAIGHT = (0,)
FAR_Z = False
MESH = pl.DeviceIdType.MESH
F32 = jnp.float32
BF16 = jnp.bfloat16


def signed(k):
    return np.where(k > NR // 2, k - NR, k)


def sphere():
    flat = np.arange(NR**3)
    comps = [signed(c) for c in (flat // NR**2, flat // NR % NR, flat % NR)]
    length = sum(c * c for c in comps)
    inside = flat[length <= np.sort(length)[NG - 1]]
    return np.unique(inside // NR**2), np.unique(inside % NR**2)


KX, COLS = sphere()


def mirrored(cols):
    return (-(cols // NR) % NR) * NR + -(cols % NR) % NR


PLUS = COLS[COLS < mirrored(COLS)][: MAIN // 2]
OTHER = np.setdiff1d(COLS, np.concatenate([PLUS, mirrored(PLUS)]))
COLS = np.concatenate([PLUS, mirrored(PLUS), OTHER])
NK = len(KX)
NC = len(COLS)
assert len(PLUS) == MAIN // 2 and len(OTHER) <= REST
ROWS = 2 * NK * VP


def split(table):
    high = table.astype(ml_dtypes.bfloat16)
    low = (table - high.astype(np.float64)).astype(ml_dtypes.bfloat16)
    return np.stack([high, low])


def plane_table():
    yz = np.arange(NR * NR)
    table = np.zeros((NR * NR, MAIN + 2 * REST))
    for cols, start, step in ((PLUS, 0, MAIN // 2), (OTHER, MAIN, REST)):
        turns = (yz // NR)[:, None] * (cols // NR)[None] + (yz % NR)[:, None] * (cols % NR)[None]
        angle = 2.0 * np.pi / NR * (turns % NR)
        table[:, start : start + len(cols)] = np.cos(angle)
        table[:, start + step : start + step + len(cols)] = np.sin(angle)
    return split(table)


def line_table():
    angle = 2.0 * np.pi / NR * (KX[:, None] * np.arange(NR)[None] % NR)
    norm = float(NR) ** -1.5
    same = np.diag(np.arange(VP) < NV)
    return split(np.concatenate([np.kron(np.cos(angle), same), np.kron(np.sin(angle), same)]) * norm)


def column_ids():
    ids = np.full((MAIN + 2 * REST,), -1, np.int32)
    ids[:NC] = COLS
    return np.ascontiguousarray(np.broadcast_to(ids[:, None], (MAIN + 2 * REST, 128)))


PLANE = plane_table()
LINE = line_table()
IDS = column_ids()


def halves(value):
    high = value.astype(BF16)
    return high, (value - high.astype(F32)).astype(BF16)


def mm(left, right):
    return jnp.dot(left, right, preferred_element_type=F32)


def kernel(
    val_hbm, cond_hbm, plane_hbm, line_hbm, ids_hbm, gvec_hbm, ve_hbm, ce_hbm, vo_hbm, co_hbm,
    out_ref,
    val_ref, cond_ref, table, line_ref, ids_ref, gvec_ref, ve_ref, ce_ref, vo_ref, co_ref,
    left_ref, right_ref, total, pair_hi, pair_lo, a_send, a_recv, hot, rho_send, scl_send, rho_recv, scl_recv,
    hear, in_sem, s1, r1, s2, r2, s3, r3, cs, cr, rs, rr,
):
    b = lax.axis_index("band")
    g = lax.axis_index("ga")
    bx, bz = b // 4, b % 4
    gl, gy, gc = g // 8, g // 2 % 4, g % 2

    def band_of(x, z):
        return lax.rem(x + 4, 4) * 4 + lax.rem(z + 4, 4)

    def ga_of(l, y, c):
        return l * 8 + lax.rem(y + 4, 4) * 2 + c

    inputs = [
        pltpu.make_async_copy(src, dst, in_sem.at[i])
        for i, (src, dst) in enumerate(
            (
                (val_hbm, val_ref),
                (cond_hbm, cond_ref),
                (plane_hbm.at[0], table.at[0]),
                (plane_hbm.at[1], table.at[1]),
                (ids_hbm, ids_ref),
                (gvec_hbm, gvec_ref),
                (line_hbm, line_ref),
                (ve_hbm, ve_ref),
                (ce_hbm, ce_ref),
                (vo_hbm, vo_ref),
                (co_hbm, co_ref),
            )
        )
    ]
    for made in inputs:
        made.start()

    barrier = pltpu.get_barrier_semaphore()

    def greet(dev):
        pl.semaphore_signal(barrier, inc=1, device_id=dev, device_id_type=MESH)

    def greet_group(d, carry):
        greet((b, lax.rem(g + d, 16)))
        return carry

    lax.fori_loop(1, 16, greet_group, 0)

    for dx, dz in ((1, 0), (-1, 0), (0, 1), (0, -1)):
        greet((band_of(bx + dx, bz + dz), g))

    def tell(step):
        for way in (1, -1):
            dev = (band_of(bx + way, bz), g) if step < 2 else (band_of(bx, bz + way), g)
            pl.semaphore_signal(hear.at[step], inc=1, device_id=dev, device_id_type=MESH)

    def heard(step):
        pl.semaphore_wait(hear.at[step], 2)

    inputs[0].wait()
    inputs[1].wait()
    row8 = lax.broadcasted_iota(jnp.int32, (VP, 1), 0)

    def valence(part, plane):
        out = jnp.zeros((VP, 1024), F32)
        for v in range(NV):
            out = jnp.where(row8 == v, val_ref[part, v].astype(F32)[plane : plane + 1], out)
        return out

    bra = [[valence(part, plane) for plane in range(2)] for part in range(2)]
    for d in range(16):
        c = lax.rem(g + 1 + d, 16)
        cre = cond_ref[0, c].astype(F32)
        cim = cond_ref[1, c].astype(F32)
        parts_re = []
        parts_im = []
        for plane in range(2):
            wre = cre[plane : plane + 1]
            wim = cim[plane : plane + 1]
            parts_re.append(bra[0][plane] * wre + bra[1][plane] * wim)
            parts_im.append(bra[0][plane] * wim - bra[1][plane] * wre)
        for part, values in enumerate((parts_re, parts_im)):
            high, low = halves(jnp.concatenate(values, axis=0))
            at = d // 8 * 256 + part * 128 + 16 * (d % 8)
            pair_hi[at : at + 16] = high
            pair_lo[at : at + 16] = low

    lane = lax.broadcasted_iota(jnp.int32, (1, 128), 1)
    sign = jnp.where(lane < REST, 1.0, -1.0).astype(F32)
    row3 = lax.broadcasted_iota(jnp.int32, (16, VP, 128), 1)

    def first(d, slot):
        return pltpu.make_async_remote_copy(
            src_ref=a_send.at[d], dst_ref=a_recv.at[slot], send_sem=s1.at[d], recv_sem=r1.at[slot],
            device_id=(b, lax.rem(g + 1 + d, 16)), device_id_type=MESH,
        )

    def send_first(d, carry):
        first(d, g).start()
        return carry

    for q in range(2):
        high = pair_hi[q * 256 : q * 256 + 256]
        if q == 0:
            inputs[2].wait()
        both = mm(high, table[0]) + mm(pair_lo[q * 256 : q * 256 + 256], table[0])
        if q == 0:
            inputs[3].wait()
        both = both + mm(high, table[1])
        yre, yim = both[:128], both[128:]
        cre, sre, cim, sim = (t[:, i * 128 : (i + 1) * 128] for t in (yre, yim) for i in range(2))
        rest = pltpu.roll(yim[:, MAIN:], REST, 1) + sign * yre[:, MAIN:]
        tiles = [t.reshape(16, VP, 128) for t in (cre + sim, cre - sim, cim - sre, cim + sre)]
        for i in range(3):
            packed = jnp.where(row3 < NV, tiles[i], pltpu.roll(tiles[3], NV - 2 * i, 1))
            a_send[8 * q : 8 * q + 8, :, i * 128 : (i + 1) * 128] = packed.reshape(8, 16, 128)
        a_send[8 * q : 8 * q + 8, :, 384:] = rest.reshape(8, 16, 128)
        if q == 0:
            pl.semaphore_wait(barrier, 19)
        lax.fori_loop(8 * q, 8 + 7 * q, send_first, 0)
        if q == 1:
            heard(0)
        tell(q)
    a_recv[g] = a_send[15]

    inputs[4].wait()
    inputs[5].wait()

    def one_hot(q, carry):
        for h in range(2):
            for i in range(2):
                yz = jnp.bitwise_and(gvec_ref[pl.ds(2 * q + 16 * i + h, 1)], NR * NR - 1)
                hot[h, q, :, i * 128 : (i + 1) * 128] = jnp.where(ids_ref[...] == yz, 1.0, 0.0).astype(BF16)
        return carry

    lax.fori_loop(0, 8, one_hot, 0)
    heard(1)
    tell(2)
    for made in inputs[6:]:
        made.wait()

    def wait_first(d, carry):
        first(d, lax.rem(g + 1 + d, 16)).wait_recv()
        return carry

    lax.fori_loop(0, 15, wait_first, 0)
    heard(2)
    tell(3)

    row3 = lax.broadcasted_iota(jnp.int32, (32, VP, 128), 1)
    tiles = [a_recv[:, :, i * 128 : (i + 1) * 128].reshape(32, VP, 128) for i in range(3)]
    last = pltpu.roll(tiles[2], 6, 1)
    for i in (1, 0):
        last = jnp.where(row3 < 2 * i + 2, pltpu.roll(tiles[i], 2 + 2 * i, 1), last)
    whole = [t.reshape(256, 128) for t in (*tiles, last)] + [a_recv[:, :, 384:].reshape(256, 128)]
    a_hi, a_lo = halves(jnp.concatenate(whole, axis=1))
    uv = mm(line_ref[0], a_hi) + mm(line_ref[0], a_lo) + mm(line_ref[1], a_hi)
    u, v = uv[: ROWS // 2], uv[ROWS // 2 :]
    rest = u[:, 2 * MAIN :] + sign * pltpu.roll(v[:, 2 * MAIN :], REST, 1)
    z_re = jnp.concatenate([u[:, :MAIN] + v[:, MAIN : 2 * MAIN], rest], axis=1)
    z_im = jnp.concatenate([u[:, MAIN : 2 * MAIN] - v[:, :MAIN], pltpu.roll(rest, REST, 1)], axis=1)
    z = jnp.concatenate([z_re, z_im], axis=0).astype(BF16)
    level = jnp.zeros((VP, 256), F32)
    filled = jnp.zeros((VP, 256), jnp.int32)
    for v in range(NV):
        level = jnp.where(row8 == v, ve_ref[v], level)
        filled = jnp.where(row8 == v, vo_ref[v], filled)
    factor = float(NV * 256) ** -0.5
    weight = (filled - co_ref[g]).astype(F32) / (level - ce_ref[g]) * factor

    def second(h, dest, slot):
        return pltpu.make_async_remote_copy(
            src_ref=rho_send.at[h, dest], dst_ref=rho_recv.at[h, slot],
            send_sem=s2.at[h, dest], recv_sem=r2.at[h, slot],
            device_id=(b, dest), device_id_type=MESH,
        )

    def third(h, dest, slot):
        return pltpu.make_async_remote_copy(
            src_ref=scl_send.at[h, dest], dst_ref=scl_recv.at[h, slot],
            send_sem=s3.at[h, dest], recv_sem=r3.at[h, slot],
            device_id=(dest, b), device_id_type=MESH,
        )

    def pick(h, d):
        q = lax.rem(g + d, 8)
        found = mm(z, hot[h, q])
        kx = jnp.concatenate([gvec_ref[pl.ds(2 * q + 16 * i + h, 1)] for i in range(2)], axis=1)
        kx = jnp.broadcast_to(jnp.right_shift(kx, 10), (VP, 256))
        re = jnp.zeros((VP, 256), F32)
        im = jnp.zeros((VP, 256), F32)
        for k in range(NK):
            here = kx == int(KX[k])
            re = jnp.where(here, found[k * VP : (k + 1) * VP], re)
            im = jnp.where(here, found[(NK + k) * VP : (NK + k + 1) * VP], im)
        rho = jnp.concatenate([re, im], axis=0).astype(BF16)
        scaled = jnp.concatenate([re * weight, im * weight], axis=0).astype(BF16)
        for i in range(2):
            rho_send[h, q + 8 * i] = rho[:, i * 128 : (i + 1) * 128]
            scl_send[h, q + 8 * i] = scaled[:, i * 128 : (i + 1) * 128]

    def send_second(h, d, carry):
        second(h, lax.rem(g + d, 16), g).start()
        return carry

    def send_third(h, d, carry):
        third(h, lax.rem(g + d, 16), g).start()
        return carry

    row = lax.broadcasted_iota(jnp.int32, (VP, 128), 0)

    def repack(src, out, h, slot):
        for part in range(2):
            groups = []
            for quad in range(4):
                four = [src[h, 4 * quad + i].astype(F32)[part * VP : (part + 1) * VP] for i in range(4)]
                for i in range(3):
                    groups.append(jnp.where(row < NV, four[i], pltpu.roll(four[3], NV - 2 * i, 0)))
            out[h, slot, part * 96 : (part + 1) * 96] = jnp.concatenate(groups, axis=0).astype(BF16)

    def wait_second(h, d, carry):
        peer = lax.rem(g + d, 16)
        second(h, peer, peer).wait_recv()
        return carry

    def wait_third(h, d, carry):
        peer = lax.rem(g + d, 16)

        @pl.when(jnp.logical_or(b != g, d != 0))
        def _():
            third(h, peer, peer).wait_recv()

        return carry

    started = []

    def copy(buf, h, slot, part, sems, role, dev):
        where = buf.at[h, slot] if part is None else buf.at[h, slot, pl.ds(part * 96, 96)]
        return pltpu.make_async_remote_copy(
            src_ref=where, dst_ref=where, send_sem=sems[0].at[h, role], recv_sem=sems[1].at[h, role],
            device_id=dev, device_id_type=MESH,
        )

    def go(*args):
        made = copy(*args)
        made.start()
        started.append(made)

    csem = (cs, cr)

    def dev_b(dx, dz):
        return (band_of(bx + dx, bz + dz), g)

    def send_x(h, n, dz):
        slot = band_of(bx, bz + dz)
        go(right_ref, h, slot, None, csem, 4 + 4 * n, dev_b(1, 0))
        go(right_ref, h, slot, None, csem, 5 + 4 * n, dev_b(-1, 0))
        if n in STRAIGHT:
            go(right_ref, h, slot, None, csem, 6 + 4 * n, dev_b(2, 0))

    def wait_c(h, slot, part, role):
        copy(right_ref, h, slot, part, csem, role, dev_b(1, 0)).wait_recv()

    def relay_x(h, n, dz):
        for part, dx in enumerate((1, -1)):
            slot = band_of(bx - dx, bz + dz)
            wait_c(h, slot, None, 4 + 4 * n + part)
            if n not in STRAIGHT:
                go(right_ref, h, slot, part, csem, 6 + 4 * n + part, dev_b(dx, 0))

    def relay_z(h):
        for part, dz in enumerate((1, -1)):
            slot = band_of(bx, bz - dz)
            wait_c(h, slot, None, part)
            if not FAR_Z:
                go(right_ref, h, slot, part, csem, 2 + part, dev_b(0, dz))
            send_x(h, 1 + part, -dz)

    def far_z(h):
        if FAR_Z:
            wait_c(h, band_of(bx, bz + 2), None, 2)
        else:
            wait_c(h, band_of(bx, bz + 2), 0, 2)
            wait_c(h, band_of(bx, bz + 2), 1, 3)
        send_x(h, 3, 2)

    rsem = (rs, rr)

    def dev_g(dl, dy, dc):
        return (b, ga_of(1 - gl if dl else gl, gy + dy, 1 - gc if dc else gc))

    def send_y(h, n):
        slot = dev_g(n, 0, 0)[1]
        for i, dy in enumerate((1, -1, 2)):
            go(left_ref, h, slot, None, rsem, 1 + 3 * n + i, dev_g(0, dy, 0))

    def wait_r(h, slot, role):
        copy(left_ref, h, slot, None, rsem, role, dev_g(0, 1, 0)).wait_recv()

    def send_core(h, n, k):
        go(left_ref, h, dev_g(n, (0, -1, 1, 2)[k], 0)[1], None, rsem, 7 + 4 * n + k, dev_g(0, 0, 1))

    def relay_l(h):
        wait_r(h, dev_g(1, 0, 0)[1], 0)
        send_y(h, 1)
        send_core(h, 1, 0)

    def relay_y(h, n):
        for k, dy in enumerate((-1, 1, 2)):
            wait_r(h, dev_g(n, dy, 0)[1], 1 + 3 * n + k)
            send_core(h, n, k + 1)

    def all_thirds(h):
        lax.fori_loop(1, 16, functools.partial(send_third, h), 0)

        @pl.when(b != g)
        def _():
            third(h, g, g).start()

        @pl.when(b == g)
        def _():
            scl_recv[h, g] = scl_send[h, g]

    for h in range(2):
        for d in range(1, 9):
            pick(h, d)
        if h == 0:
            heard(3)
        all_thirds(h)
        lax.fori_loop(1, 16, functools.partial(send_second, h), 0)
        rho_recv[h, g] = rho_send[h, g]

    def rows(h):
        lax.fori_loop(0, 16, functools.partial(wait_third, h), 0)
        repack(scl_recv, left_ref, h, g)
        go(left_ref, h, g, None, rsem, 0, dev_g(1, 0, 0))
        send_y(h, 0)
        send_core(h, 0, 0)

    for h in range(2):
        lax.fori_loop(1, 16, functools.partial(wait_second, h), 0)
        repack(rho_recv, right_ref, h, b)
        go(right_ref, h, b, None, csem, 0, dev_b(0, 1))
        go(right_ref, h, b, None, csem, 1, dev_b(0, -1))
        if FAR_Z:
            go(right_ref, h, b, None, csem, 2, dev_b(0, 2))
        send_x(h, 0, 0)
    for h in range(2):
        rows(h)
        relay_z(h)
    relay_l(0)
    relay_l(1)
    for h in range(2):
        relay_x(h, 1, -1)
        relay_x(h, 2, 1)
        far_z(h)
        relay_y(h, 0)
    for h in range(2):
        relay_y(h, 1)
        relay_x(h, 3, 2)
    for h in range(2):
        for n in range(2):
            for k, dy in enumerate((0, -1, 1, 2)):
                wait_r(h, dev_g(n, dy, 1)[1], 7 + 4 * n + k)

    for h in range(2):
        relay_x(h, 0, 0)
    dims = (((0,), (0,)), ((), ()))
    for n, dz in enumerate((0, -1, 1, 2)):
        for h in range(2):
            if n in STRAIGHT:
                wait_c(h, band_of(bx + 2, bz + dz), None, 6 + 4 * n)
            else:
                for part in range(2):
                    wait_c(h, band_of(bx + 2, bz + dz), part, 6 + 4 * n + part)
        slots = [band_of(x, bz + dz) for x in range(4)]
        left = jnp.concatenate([jnp.concatenate([left_ref[h, k] for k in slots], axis=0) for h in range(2)], axis=1)
        right = jnp.concatenate([jnp.concatenate([right_ref[h, k] for k in slots], axis=0) for h in range(2)], axis=1)
        turned = jnp.concatenate(
            [t for k in range(4) for t in (-right[192 * k + 96 : 192 * k + 192], right[192 * k : 192 * k + 96])], axis=0
        )
        for part, other in enumerate((right, turned)):
            value = lax.dot_general(left, other, dims, preferred_element_type=F32)
            if n == 0:
                total[part] = value
            elif n < 3:
                total[part] += value
            else:
                out_ref[:, part, :] = total[part] + value

    for made in started:
        made.wait_send()

    def drain(d, carry):
        first(d - 1, g).wait_send()
        for h in range(2):
            second(h, lax.rem(g + d, 16), g).wait_send()
        return carry

    lax.fori_loop(1, 16, drain, 0)

    def drain_third(d, carry):
        dest = lax.rem(b + d, 16)

        @pl.when(jnp.logical_or(b != g, d != 0))
        def _():
            for h in range(2):
                third(h, dest, g).wait_send()

        return carry

    lax.fori_loop(0, 16, drain_third, 0)


def body(
    valence_waves,
    conduction_waves,
    valence_energy,
    conduction_energy,
    valence_occupied,
    conduction_occupied,
    gvec_index,
):
    vmem = pl.BlockSpec(memory_space=pltpu.VMEM)
    hbm = pl.BlockSpec(memory_space=pltpu.HBM)
    dma = pltpu.SemaphoreType.DMA
    return pl.pallas_call(
        kernel,
        out_shape=jax.ShapeDtypeStruct((256, 2, 256), F32),
        in_specs=[hbm] * 10,
        out_specs=vmem,
        scratch_shapes=[
            pltpu.VMEM(valence_waves.shape, BF16),
            pltpu.VMEM(conduction_waves.shape, BF16),
            pltpu.VMEM(PLANE.shape, BF16),
            pltpu.VMEM(LINE.shape, BF16),
            pltpu.VMEM(IDS.shape, jnp.int32),
            pltpu.VMEM((32, 128), jnp.int32),
            pltpu.SMEM((NV,), F32),
            pltpu.SMEM((16,), F32),
            pltpu.SMEM((NV,), jnp.int32),
            pltpu.SMEM((16,), jnp.int32),
            pltpu.VMEM((2, 16, 192, 128), BF16),
            pltpu.VMEM((2, 16, 192, 128), BF16),
            pltpu.VMEM((2, 256, 256), F32),
            pltpu.VMEM((512, 1024), BF16),
            pltpu.VMEM((512, 1024), BF16),
            pltpu.VMEM((16, 16, 512), F32),
            pltpu.VMEM((16, 16, 512), F32),
            pltpu.VMEM((2, 8, MAIN + 2 * REST, 256), BF16),
            pltpu.VMEM((2, 16, 16, 128), BF16),
            pltpu.VMEM((2, 16, 16, 128), BF16),
            pltpu.VMEM((2, 16, 16, 128), BF16),
            pltpu.VMEM((2, 16, 16, 128), BF16),
            pltpu.SemaphoreType.REGULAR((4,)),
            dma((11,)),
            dma((16,)),
            dma((16,)),
            dma((2, 16)),
            dma((2, 16)),
            dma((2, 16)),
            dma((2, 16)),
            dma((2, 20)),
            dma((2, 20)),
            dma((2, 15)),
            dma((2, 15)),
        ],
        compiler_params=pltpu.CompilerParams(
            collective_id=0, has_side_effects=True, vmem_limit_bytes=60 * 1024 * 1024
        ),
        name="pairs",
    )(
        valence_waves, conduction_waves, jnp.asarray(PLANE), jnp.asarray(LINE), jnp.asarray(IDS),
        gvec_index.reshape(32, 128), valence_energy, conduction_energy, valence_occupied, conduction_occupied,
    )


def solution(mesh):
    placed = (
        P(None, None, "ga", None),
        P(None, "band", "ga", None),
        P(),
        P("band"),
        P(),
        P("band"),
        P(),
    )
    return jax.shard_map(
        body, mesh=mesh, in_specs=placed, out_specs=P("band", None, "ga"), check_vma=False
    )
```
